128 devices in a mesh: fsdp: 16 (over z_hi, y, core), seq: 8 (over z_lo, x).
Axes of the slice: x: 4, y: 4, z: 4 (z_hi: 2, z_lo: 2; z = z_hi * 2 + z_lo), core: 2. Of those that a mesh axis runs over, the one named last changes fastest.
Arguments:
- tokens: bfloat16 [2048, 8192], P('seq', 'fsdp'), may hold values from -6 to 6
- lang_ids: int32 [2048], P('seq'), may hold values from 0 to 1
- norm_gain: float32 [8192], replicated, may hold values from 0.1 to 1.9
- gate_weight: bfloat16 [8192, 12288], P('seq', 'fsdp'), may hold values from -0.0625 to 0.0625
- up_weight: bfloat16 [8192, 12288], P('seq', 'fsdp'), may hold values from -0.0625 to 0.0625
Outputs:
- gram_in: float32 [8192, 8192], P('fsdp', 'seq')
- gram_hidden: float32 [12288, 12288], P('fsdp', 'seq')
The draws below stay inside these ranges and needn't reach their ends.
All inputs are finite; a program needn't handle non-finite values.
Results may differ from the reference program's by a relative error of at most 0.0068.
Values may be sent and summed in bfloat16 or wider, within the bound.
A program may use at most 128 MiB of HBM per device.

```python
import jax
import jax.numpy as jnp
from jax import lax

D = 8192
FFW = 12288
TOKENS = 2048


def with_ends(values, rng, smallest, high):
    index_at = [jax.random.randint(jax.random.fold_in(rng, axis), (), 0, length) for axis, length in enumerate(values.shape)]
    longest = values.shape.index(max(values.shape))
    next_to = index_at[:longest] + [(index_at[longest] + 1) % values.shape[longest]] + index_at[longest + 1:]
    return values.at[tuple(index_at)].set(smallest).at[tuple(next_to)].set(high)


def shard_levels(own_key, dims, shards, smallest, high):
    level = 1.0
    for dim, parts in shards:
        draws = jax.random.uniform(jax.random.fold_in(jax.random.fold_in(own_key, 6), dim), (parts,), jnp.float32, smallest / len(shards), high / len(shards))
        level = level * jnp.repeat(jnp.exp(draws), dims[dim] // parts).reshape((-1,) + (1,) * (len(dims) - 1 - dim))
    return level


def noise(key, extent, spread, reach, split=(), held_as=jnp.bfloat16):
    entries = spread * jax.random.normal(key, extent, jnp.float32)
    if split:
        entries = entries * shard_levels(key, extent, split, -0.22, 0.18)
    return jnp.clip(entries, -reach, reach).astype(held_as)


def setup_inputs(seed: int = 0) -> dict:
    seeds = jax.random.split(jax.random.key(seed), 6)
    tokens = noise(seeds[0], (TOKENS, D), 1.0, 6.0, ((0, 8), (1, 16)))
    lang_ids = with_ends(jax.random.randint(seeds[1], (TOKENS,), 0, 2), jax.random.fold_in(seeds[1], 1), 0, 1).astype(jnp.int32)
    norm_gain = jnp.clip(1.0 + 0.18 * jax.random.normal(seeds[2], (D,), jnp.float32), 0.1, 1.9)
    gate_weight = noise(seeds[3], (D, FFW), D ** -0.5, 0.0625, ((0, 8), (1, 16)))
    up_weight = noise(seeds[4], (D, FFW), D ** -0.5, 0.0625, ((0, 8), (1, 16)))
    return dict(tokens=tokens, lang_ids=lang_ids, norm_gain=norm_gain, gate_weight=gate_weight, up_weight=up_weight)


def reference(tokens, lang_ids, norm_gain, gate_weight, up_weight):
    values = tokens.astype(jnp.float32)
    scale = jax.lax.rsqrt(lax.optimization_barrier(jnp.mean(values * values, axis=1, keepdims=True)) + 1e-05)
    normed = (values * scale * norm_gain.astype(jnp.float32)[None, :]).astype(jnp.bfloat16)
    keep = (lang_ids == 0).astype(jnp.bfloat16)[:, None]
    gate = jnp.dot(normed, gate_weight, preferred_element_type=jnp.float32)
    up = jnp.dot(normed, up_weight, preferred_element_type=jnp.float32)
    hidden = (jax.nn.silu(gate) * up).astype(jnp.bfloat16)
    masked_in = normed * keep
    masked_hidden = hidden * keep
    gram_in = jnp.dot(masked_in.T, masked_in, preferred_element_type=jnp.float32) / TOKENS
    gram_hidden = jnp.dot(masked_hidden.T, masked_hidden, preferred_element_type=jnp.float32) / TOKENS
    return (gram_in, gram_hidden)
```

```python
import functools

import jax
import jax.numpy as jnp
from jax import lax
from jax.experimental import pallas as pl
from jax.experimental.pallas import tpu as pltpu
from jax.sharding import PartitionSpec as P

MESH = pl.DeviceIdType.MESH
F32 = jnp.float32
BF16 = jnp.bfloat16
TOK = 256
FEAT = 512
COLS = 768
WA, WB = 512, 256
DEPTH = 1024
TOTAL = 2048
D = 8192

_RANGES = {}
_next = 0
for _name, _count in (
    ("z", 3), ("ss", 8), ("rsa", 4), ("rsb", 4), ("rsa2", 4), ("rsb2", 1),
    ("Xcy", 4), ("Xrx", 4), ("Xax", 4), ("Xsib", 4), ("Xrz", 4),
    ("Az", 3), ("Acy", 4), ("Arx", 4), ("Aax", 4), ("Asib", 4), ("Arz", 4),
    ("Bz", 3), ("Bcy", 4), ("Brx", 4), ("Bax", 4), ("Bsib", 4), ("Brz", 4),
):
    _RANGES[_name] = _next
    _next += _count
N_SEM = _next


def mod4(v):
    return lax.rem(v + 8, 4)


def kernel(
    tok_ref, gain_ref, wg_hbm, wu_hbm,
    xf_out, xs_out, hf_out, hs_out,
    raw, nb, ss, xc, xf, xs, wg, wu, pa, pb, ra, ra2, rb, rb2, sbf,
    hba, hca, hfa, hsa, hbb, hcb, hfb, hsb,
    ssem, rsem, wsem, osem,
):
    f = lax.axis_index("fsdp")
    s = lax.axis_index("seq")
    zh, y, c = f // 8, lax.rem(f // 2, 4), lax.rem(f, 2)
    zl, x = s // 4, lax.rem(s, 4)

    def dev(zh_, y_, c_, zl_, x_):
        return (zh_ * 8 + y_ * 2 + c_, zl_ * 4 + x_)

    z_src = [(zh, 1 - zl), (1 - zh, zl), (1 - zh, 1 - zl)]
    z_peers = [dev(a, y, c, b, x) for a, b in z_src]
    partner = z_peers[0]
    sib = dev(zh, y, 1 - c, zl, x)

    def x_peer(d):
        return dev(zh, y, c, zl, mod4(x + d))

    def y_peer(d, e=0):
        return dev(zh, mod4(y + d), c if e == 0 else 1 - c, zl, x)

    pending = []

    def remote(src, dst, name, i, device):
        base = _RANGES[name]
        return pltpu.make_async_remote_copy(
            src_ref=src, dst_ref=dst, send_sem=ssem.at[base + i], recv_sem=rsem.at[base + i],
            device_id=device, device_id_type=MESH,
        )

    def send(src, dst, name, i, device):
        copy = remote(src, dst, name, i, device)
        copy.start()
        pending.append(copy)

    def arrived(dst, name, i):
        remote(dst, dst, name, i, sib).wait_recv()

    w_copies = [
        pltpu.make_async_copy(wg_hbm, wg, wsem.at[0]),
        pltpu.make_async_copy(wu_hbm, wu, wsem.at[1]),
    ]
    for copy in w_copies:
        copy.start()

    barrier = pltpu.get_barrier_semaphore()
    peers = list(z_peers) + [x_peer(d) for d in (1, 2, 3)]
    peers += [y_peer(d, e) for d in range(4) for e in range(2) if (d, e) != (0, 0)]
    for peer in peers:
        pl.semaphore_signal(barrier, inc=1, device_id=peer, device_id_type=MESH)
    raw[zh, zl] = tok_ref[...]
    pl.semaphore_wait(barrier, len(peers))

    for i, peer in enumerate(z_peers):
        send(raw.at[zh, zl], raw.at[zh, zl], "z", i, peer)
    for i, (a, b) in enumerate(z_src):
        arrived(raw.at[a, b], "z", i)

    slot = y * 2 + c
    for t in range(2):
        v0 = raw[0, t].astype(F32)
        v1 = raw[1, t].astype(F32)
        sq = v0 * v0 + v1 * v1
        sq = sq[:, 0:128] + sq[:, 128:256] + sq[:, 256:384] + sq[:, 384:512]
        row = jnp.sum(jnp.transpose(sq), axis=0, keepdims=True)
        ss[slot, :, t * TOK:(t + 1) * TOK] = jnp.broadcast_to(row, (8, TOK))
    for d in range(4):
        for e in range(2):
            if (d, e) != (0, 0):
                send(ss.at[slot], ss.at[slot], "ss", d * 2 + e, y_peer(d, e))
    for d in range(4):
        for e in range(2):
            if (d, e) != (0, 0):
                arrived(ss.at[mod4(y - d) * 2 + (c if e == 0 else 1 - c)], "ss", d * 2 + e)
    total = ss[0]
    for i in range(1, 8):
        total = total + ss[i]
    scale = lax.rsqrt(total / float(D) + 1e-05)
    for t in range(2):
        col = jnp.transpose(jnp.broadcast_to(scale[0:1, t * TOK:(t + 1) * TOK], (128, TOK)))
        for b in range(2):
            g = gain_ref[b * 8 + y * 2 + c]
            for k in range(FEAT // 128):
                lanes = slice(k * 128, (k + 1) * 128)
                v = raw[b, t, :, lanes].astype(F32)
                nb[b, t, :, lanes] = (v * col * g[:, lanes]).astype(BF16)

    def row_first(q, own, row):
        for d in (1, 3, 2):
            send(own.at[zh, zl], row.at[x, zl], q + "rx", d, x_peer(d))

    def column_first(q, own, col):
        for d in (1, 3, 2):
            send(own.at[zl], col.at[y], q + "cy", d, y_peer(d))
        col[y] = own[zl]

    def column_wait(q, col, yy):
        d = mod4(y - yy)

        @pl.when(d != 0)
        def _():
            arrived(col.at[yy], q + "cy", d)

    def column_second(q, col, panel):
        for d in (1, 3, 2):
            to = mod4(x + d)
            column_wait(q, col, to)
            send(col.at[to], panel.at[c, x], q + "ax", d, x_peer(d))
        column_wait(q, col, x)
        send(col.at[x], panel.at[c, x], q + "sib", 0, sib)
        panel[c, x] = col[x]

    def column_third(q, panel, d):
        at = mod4(x - d)
        arrived(panel.at[c, at], q + "ax", d)
        send(panel.at[c, at], panel.at[c, at], q + "sib", d, sib)

    def column_done(q, panel, d):
        arrived(panel.at[1 - c, mod4(x - d)], q + "sib", d)

    def row_second(q, own, row):
        row[x] = own[zh]
        for d in (1, 3, 2):
            at = mod4(x - d)
            arrived(row.at[at, zl], q + "rx", d)
            send(row.at[at, zl], row.at[at, zl], q + "rz", d, partner)

    def row_done(q, row):
        for d in (1, 3, 2):
            arrived(row.at[mod4(x - d), 1 - zl], q + "rz", d)

    column_first("X", nb, xc)
    row_first("X", nb, xf)
    column_second("X", xc, xs)
    row_second("X", nb, xf)
    for copy in w_copies:
        copy.wait()

    for d in (0, 1, 3, 2):
        if d:
            column_third("X", xs, d)
        column_done("X", xs, d)
        at = mod4(x - d)

        def half(t, _):
            a0 = xs[0, at, t]
            a1 = xs[1, at, t]

            def product(w, n):
                lanes = slice(n * 256, (n + 1) * 256)
                return (
                    jnp.dot(a0, w[0:FEAT, lanes], preferred_element_type=F32)
                    + jnp.dot(a1, w[FEAT:DEPTH, lanes], preferred_element_type=F32)
                ).astype(BF16)

            for n in range(2):
                pa[at, t, :, n * 256:(n + 1) * 256] = product(wg, n)
                pa[at, t, :, WA + n * 256:WA + (n + 1) * 256] = product(wu, n)
            pb[at, t, :, 0:WB] = product(wg, 2)
            pb[at, t, :, WB:2 * WB] = product(wu, 2)
            return 0

        lax.fori_loop(0, 2, half, 0)
        send(pa.at[at, 1 - zl], ra.at[at], "rsa", d, partner)
        if d:
            send(pb.at[at], rb.at[x], "rsb", 4 - d, dev(zh, y, c, zl, at))

    row_done("X", xf)
    outs = []

    def store(src, dst):
        copy = pltpu.make_async_copy(src, dst, osem.at[len(outs)])
        copy.start()
        outs.append(copy)

    store(xf, xf_out)
    for cc in range(2):
        store(xs.at[cc], xs_out.at[:, :, :, pl.ds(cc * FEAT, FEAT)])

    def second(d):
        at = mod4(x - d)
        arrived(ra.at[at], "rsa", d)
        if d:
            pa[at, zl] = (pa[at, zl].astype(F32) + ra[at].astype(F32)).astype(BF16)
            send(pa.at[at, zl], ra2.at[x], "rsa2", 4 - d, dev(zh, y, c, zl, at))

    def swiglu(v, w):
        g, u = v[:, 0:w], v[:, w:2 * w]
        return (g / (1.0 + jnp.exp(-g)) * u).astype(BF16)

    second(0)
    second(1)
    for d in (1, 3, 2):
        arrived(rb.at[mod4(x - d)], "rsb", d)

    def sum_b(t):
        v = pb[x, t].astype(F32)
        for d in (1, 2, 3):
            v = v + rb[mod4(x - d), t].astype(F32)
        return v

    sbf[...] = sum_b(1 - zl).astype(BF16)
    send(sbf, rb2, "rsb2", 0, partner)
    second(3)
    second(2)
    arrived(rb2, "rsb2", 0)
    hbb[zh, zl] = swiglu(sum_b(zl) + rb2[...].astype(F32), WB)

    def z_send(q, own):
        for i, peer in enumerate(z_peers):
            send(own.at[zh, zl], own.at[zh, zl], q + "z", i, peer)

    def z_wait(q, own):
        for i, (a, b) in enumerate(z_src):
            arrived(own.at[a, b], q + "z", i)

    z_send("B", hbb)
    row_first("B", hbb, hfb)

    for d in (1, 3, 2):
        arrived(ra2.at[mod4(x - d)], "rsa2", d)
    va = pa[x, zl].astype(F32) + ra[x].astype(F32)
    for d in (1, 2, 3):
        va = va + ra2[mod4(x - d)].astype(F32)
    hba[zh, zl] = swiglu(va, WA)
    z_send("A", hba)
    row_first("A", hba, hfa)

    z_wait("B", hbb)
    column_first("B", hbb, hcb)
    z_wait("A", hba)
    column_first("A", hba, hca)
    column_second("B", hcb, hsb)
    row_second("B", hbb, hfb)
    column_second("A", hca, hsa)
    row_second("A", hba, hfa)
    for d in (1, 3, 2):
        column_third("B", hsb, d)
    for d in (0, 1, 3, 2):
        column_done("B", hsb, d)
    row_done("B", hfb)
    store(hfb, hf_out.at[:, :, :, pl.ds(WA, WB)])
    for cc in range(2):
        store(hsb.at[cc], hs_out.at[:, :, :, pl.ds(cc * COLS + WA, WB)])
    for d in (1, 3, 2):
        column_third("A", hsa, d)
    for d in (0, 1, 3, 2):
        column_done("A", hsa, d)
    row_done("A", hfa)
    store(hfa, hf_out.at[:, :, :, pl.ds(0, WA)])
    for cc in range(2):
        store(hsa.at[cc], hs_out.at[:, :, :, pl.ds(cc * COLS, WA)])
    for copy in pending:
        copy.wait_send()
    for copy in outs:
        copy.wait()


def panels(tokens, gain, gate_weight, up_weight):
    def vm(*shape, dtype=BF16):
        return pltpu.VMEM(shape, dtype)

    shapes = [(4, 2, TOK, FEAT), (4, 2, TOK, 2 * FEAT), (4, 2, TOK, COLS), (4, 2, TOK, 2 * COLS)]
    any_spec = pl.BlockSpec(memory_space=pl.ANY)
    vmem_spec = pl.BlockSpec(memory_space=pltpu.VMEM)
    scratch = [
        vm(2, 2, TOK, FEAT), vm(2, 2, TOK, FEAT), vm(8, 8, 2 * TOK, dtype=F32),
        vm(4, 2, TOK, FEAT), vm(4, 2, TOK, FEAT), vm(2, 4, 2, TOK, FEAT),
        vm(DEPTH, COLS), vm(DEPTH, COLS),
        vm(4, 2, TOK, 2 * WA), vm(4, 2, TOK, 2 * WB), vm(4, TOK, 2 * WA), vm(4, TOK, 2 * WA),
        vm(4, 2, TOK, 2 * WB), vm(TOK, 2 * WB), vm(TOK, 2 * WB),
    ]
    for w in (WA, WB):
        scratch += [vm(2, 2, TOK, w), vm(4, 2, TOK, w), vm(4, 2, TOK, w), vm(2, 4, 2, TOK, w)]
    scratch += [
        pltpu.SemaphoreType.DMA((N_SEM,)), pltpu.SemaphoreType.DMA((N_SEM,)),
        pltpu.SemaphoreType.DMA((2,)), pltpu.SemaphoreType.DMA((9,)),
    ]
    return pl.pallas_call(
        kernel,
        out_shape=[jax.ShapeDtypeStruct(shape, BF16) for shape in shapes],
        in_specs=[vmem_spec, vmem_spec, any_spec, any_spec],
        out_specs=[any_spec] * 4,
        scratch_shapes=scratch,
        compiler_params=pltpu.CompilerParams(
            collective_id=0, has_side_effects=True, vmem_limit_bytes=56 * 2**20
        ),
        cost_estimate=pl.CostEstimate(flops=2 * 2048 * 1024 * 1536, bytes_accessed=20 * 2**20, transcendentals=0),
    )(tokens, gain, gate_weight, up_weight)


def gram(left, right):
    left = left.reshape(TOTAL, left.shape[-1])
    right = right.reshape(TOTAL, right.shape[-1])
    return lax.dot_general(
        left, right, (((0,), (0,)), ((), ())), preferred_element_type=F32
    ) / float(TOTAL)


def per_device(tokens, lang_ids, norm_gain, gate_weight, up_weight):
    masked = jnp.where((lang_ids == 0)[:, None], tokens, jnp.zeros_like(tokens))
    xf, xs, hf, hs = panels(masked, norm_gain.reshape(16, 1, FEAT), gate_weight, up_weight)
    return (gram(xf, xs), gram(hf, hs))


def solution(mesh):
    in_specs = (P("seq", "fsdp"), P("seq"), P(), P("seq", "fsdp"), P("seq", "fsdp"))
    out_specs = (P("fsdp", "seq"), P("fsdp", "seq"))
    return jax.shard_map(
        per_device, mesh=mesh, in_specs=in_specs, out_specs=out_specs, check_vma=False
    )
```

```python
import jax
import jax.numpy as jnp
from jax import lax
from jax.experimental import pallas as pl
from jax.experimental.pallas import tpu as pltpu
from jax.sharding import PartitionSpec as P

MESH = pl.DeviceIdType.MESH
F32 = jnp.float32
BF16 = jnp.bfloat16
TOK = 256
FEAT = 512
COLS = 768
WA, WB = 512, 256
DEPTH = 1024
TOTAL = 2048
D = 8192
NH = 4
R = TOK // NH
ORDER = (
    "ZW:0", "ZW:1", "SC:0", "ZW:2", "SC:1", "R2:0", "C2:0", "ZW:3", "SC:2", "R2:1", "R3:0", "P:0:0", "SC:3",
    "C3:0:1", "C2:1", "C3:0:3", "P:0:1", "C3:0:2", "R2:2", "P:1:0", "C2:2", "P:0:3", "S:0:0", "P:0:2", "C3:1:1",
    "C3:1:3", "S:0:1", "C2:3", "P:2:0", "C3:1:2", "P:1:1", "P:1:3", "P:3:0", "S:1:0", "C3:2:1", "P:1:2",
    "C3:2:3", "S:0:3", "R3:1", "R2:3", "R3:2", "GX:0", "C3:2:2", "P:2:1", "S:0:2", "P:2:3", "P:2:2", "S:2:0",
    "SB:0", "S:1:1", "C3:3:1", "C3:3:3", "S:1:3", "P:3:1", "C3:3:2", "P:3:3", "S:3:0", "P:3:2", "S:1:2", "GX:1",
    "SB:1", "R3:3", "GX:2", "S:2:1", "S:2:3", "SB:2", "S:2:2", "HID:0", "S:3:1", "SB:3", "S:3:3", "S:3:2",
    "HID:1", "GX:3", "HID:2", "HZ:0", "HR2:0", "HID:3", "HZ:1", "HR2:1", "HZ:2", "HR2:2", "HR3:0", "HC2:0",
    "HR3:1", "HR3:2", "HC3:0:1", "HZ:3", "HR2:3", "HC3:0:3", "HC2:1", "HC3:0:2", "HR3:3", "HC3:1:1", "HC3:1:3",
    "HC2:2", "HL:0", "HC3:1:2", "HC3:2:1", "HL:1", "HC3:2:3", "HC2:3", "HC3:2:2", "HC3:3:1", "HL:2", "HC3:3:3",
    "HC3:3:2", "HL:3",
)

_RANGES = {}
_next = 0
for _name, _count in (
    ("z", 3), ("ss", 8), ("rsa", 4), ("rsb", 4), ("rsa2", 4), ("rsb2", 1),
    ("Xcy", 4), ("Xrx", 4), ("Xax", 4), ("Xsib", 4), ("Xrz", 4),
    ("Hz", 3), ("Hcy", 4), ("Hrx", 4), ("Hax", 4), ("Hsib", 4), ("Hrz", 4),
):
    _RANGES[_name] = _next
    _next += _count
PER_PART = _next


def mod4(v):
    return lax.rem(v + 8, 4)


def kernel(
    tok_ref, lang_ref, gain_ref, wg_hbm, wu_hbm,
    gin_out, ghid_out,
    raw, nb, ss, scol, xc, xf, xs, wg, wu, pa, pb, ra, ra2, rb, rb2, sbf,
    hb, hc, hf, hs, xft, hft, gin, ghid,
    ssem, rsem, wsem, osem,
):
    f = lax.axis_index("fsdp")
    s = lax.axis_index("seq")
    zh, y, c = f // 8, lax.rem(f // 2, 4), lax.rem(f, 2)
    zl, x = s // 4, lax.rem(s, 4)

    def dev(zh_, y_, c_, zl_, x_):
        return (zh_ * 8 + y_ * 2 + c_, zl_ * 4 + x_)

    z_src = [(zh, 1 - zl), (1 - zh, zl), (1 - zh, 1 - zl)]
    z_peers = [dev(a, y, c, b, x) for a, b in z_src]
    partner = z_peers[0]
    sib = dev(zh, y, 1 - c, zl, x)

    def x_peer(d):
        return dev(zh, y, c, zl, mod4(x + d))

    def y_peer(d, e=0):
        return dev(zh, mod4(y + d), c if e == 0 else 1 - c, zl, x)

    pending = []
    outs = []

    def remote(src, dst, h, name, i, device):
        at = h * PER_PART + _RANGES[name] + i
        return pltpu.make_async_remote_copy(
            src_ref=src, dst_ref=dst, send_sem=ssem.at[at], recv_sem=rsem.at[at],
            device_id=device, device_id_type=MESH,
        )

    def send(src, dst, h, name, i, device):
        copy = remote(src, dst, h, name, i, device)
        copy.start()
        pending.append(copy)

    def arrived(dst, h, name, i):
        remote(dst, dst, h, name, i, sib).wait_recv()

    w_copies = [
        pltpu.make_async_copy(wg_hbm, wg, wsem.at[0]),
        pltpu.make_async_copy(wu_hbm, wu, wsem.at[1]),
    ]
    for copy in w_copies:
        copy.start()

    barrier = pltpu.get_barrier_semaphore()
    peers = list(z_peers) + [x_peer(d) for d in (1, 2, 3)]
    peers += [y_peer(d, e) for d in range(4) for e in range(2) if (d, e) != (0, 0)]
    for peer in peers:
        pl.semaphore_signal(barrier, inc=1, device_id=peer, device_id_type=MESH)
    keep = (lang_ref[...] == 0).astype(F32)
    for i in range(TOK // 128):
        col = jnp.transpose(jnp.broadcast_to(keep[i:i + 1], (128, 128)))
        for k in range(FEAT // 128):
            lanes = slice(k * 128, (k + 1) * 128)
            v = (tok_ref[i * 128:(i + 1) * 128, lanes].astype(F32) * col).astype(BF16)
            for j in range(128 // R):
                raw[i * (128 // R) + j, zh, zl, :, lanes] = v[j * R:(j + 1) * R]
    pl.semaphore_wait(barrier, len(peers))

    def z_send(h, name, own):
        for i, peer in enumerate(z_peers):
            send(own.at[h, zh, zl], own.at[h, zh, zl], h, name, i, peer)

    def z_wait(h, name, own):
        for i, (a, b) in enumerate(z_src):
            arrived(own.at[h, a, b], h, name, i)

    slot = y * 2 + c

    def squares(h):
        v0 = raw[h, 0].reshape(2 * R, FEAT).astype(F32)
        v1 = raw[h, 1].reshape(2 * R, FEAT).astype(F32)
        sq = v0 * v0 + v1 * v1
        sq = sq[:, 0:128] + sq[:, 128:256] + sq[:, 256:384] + sq[:, 384:512]
        row = jnp.sum(jnp.transpose(sq), axis=0, keepdims=True)
        ss[h, slot] = jnp.broadcast_to(row, (8, 2 * R))
        for d in range(4):
            for e in range(2):
                if (d, e) != (0, 0):
                    send(ss.at[h, slot], ss.at[h, slot], h, "ss", d * 2 + e, y_peer(d, e))

    def scales(h):
        for d in range(4):
            for e in range(2):
                if (d, e) != (0, 0):
                    at = mod4(y - d) * 2 + (c if e == 0 else 1 - c)
                    arrived(ss.at[h, at], h, "ss", d * 2 + e)
        total = ss[h, 0]
        for i in range(1, 8):
            total = total + ss[h, i]
        scale = lax.rsqrt(total / float(D) + 1e-05)
        scol[h] = jnp.transpose(jnp.broadcast_to(scale[0:1], (128, 2 * R)))

    def normalize(h, src, dst, b, yy):
        g = gain_ref[b * 8 + yy * 2 + c]
        col = scol[h]
        for k in range(FEAT // 128):
            lanes = slice(k * 128, (k + 1) * 128)
            v = src[:, :, lanes].reshape(2 * R, 128).astype(F32)
            dst[:, :, lanes] = (v * col * g[:, lanes]).astype(BF16).reshape(2, R, 128)

    def row_first(h, q, own, row):
        for d in (1, 3):
            send(own.at[zl], row.at[h, x, zl], h, q + "rx", d, x_peer(d))

    def column_first(h, q, own, col):
        for d in (1, 3, 2):
            send(own.at[h, zl], col.at[h, y], h, q + "cy", d, y_peer(d))
        col[h, y] = own[h, zl]

    def column_wait(h, q, col, yy):
        d = mod4(y - yy)

        @pl.when(d != 0)
        def _():
            arrived(col.at[h, yy], h, q + "cy", d)

        if q == "X":
            normalize(h, col.at[h, yy], col.at[h, yy], zl, yy)

    def column_second(h, q, col, panel):
        for d in (1, 3, 2):
            to = mod4(x + d)
            column_wait(h, q, col, to)
            send(col.at[h, to], panel.at[h, c, x], h, q + "ax", d, x_peer(d))
        column_wait(h, q, col, x)
        send(col.at[h, x], panel.at[h, c, x], h, q + "sib", 0, sib)
        panel[h, c, x] = col[h, x]

    def column_third(h, q, panel, d):
        at = mod4(x - d)
        arrived(panel.at[h, c, at], h, q + "ax", d)
        send(panel.at[h, c, at], panel.at[h, c, at], h, q + "sib", d, sib)

    def column_done(h, q, panel, d):
        arrived(panel.at[h, 1 - c, mod4(x - d)], h, q + "sib", d)

    def row_second(h, q, own, row):
        row[h, x] = own[...]
        for d, half in ((1, 0), (3, 1)):
            at = mod4(x - d)
            arrived(row.at[h, at, zl], h, q + "rx", d)
            rows = pl.ds(half * (R // 2), R // 2)
            send(row.at[h, at, zl, rows], row.at[h, at, zl, rows], h, q + "rx", 2 * half, x_peer(d))
            send(row.at[h, at, zl], row.at[h, at, zl], h, q + "rz", d, partner)

    def row_third(h, q, row):
        at = mod4(x - 2)
        for half in range(2):
            arrived(row.at[h, at, zl, pl.ds(half * (R // 2), R // 2)], h, q + "rx", 2 * half)
        send(row.at[h, at, zl], row.at[h, at, zl], h, q + "rz", 2, partner)

    def row_done(h, q, row):
        for d in (1, 3, 2):
            arrived(row.at[h, mod4(x - d), 1 - zl], h, q + "rz", d)

    def products(h, d):
        column_done(h, "X", xs, d)
        at = mod4(x - d)
        a0 = xs[h, 0, at].reshape(2 * R, FEAT)
        a1 = xs[h, 1, at].reshape(2 * R, FEAT)

        def product(w, lanes):
            v = jnp.dot(a0, w[0:FEAT, lanes], preferred_element_type=F32)
            v = v + jnp.dot(a1, w[FEAT:DEPTH, lanes], preferred_element_type=F32)
            return v.astype(BF16).reshape(2, R, 256)

        def step(n, _):
            here = pl.ds(pl.multiple_of(n * 256, 256), 256)
            there = pl.ds(pl.multiple_of(WA + n * 256, 256), 256)
            pa[h, at, :, :, here] = product(wg, here)
            pa[h, at, :, :, there] = product(wu, here)
            return 0

        lax.fori_loop(0, WA // 256, step, 0)
        send(pa.at[h, at, 1 - zl], ra.at[h, at], h, "rsa", d, partner)
        pb[h, at, :, :, 0:WB] = product(wg, slice(WA, COLS))
        pb[h, at, :, :, WB:2 * WB] = product(wu, slice(WA, COLS))
        if d:
            send(pb.at[h, at], rb.at[h, x], h, "rsb", 4 - d, dev(zh, y, c, zl, at))

    def second(h, d):
        at = mod4(x - d)
        arrived(ra.at[h, at], h, "rsa", d)
        if d:
            pa[h, at, zl] = (pa[h, at, zl].astype(F32) + ra[h, at].astype(F32)).astype(BF16)
            send(pa.at[h, at, zl], ra2.at[h, x], h, "rsa2", 4 - d, dev(zh, y, c, zl, at))

    def swiglu(v, w):
        g, u = v[:, 0:w], v[:, w:2 * w]
        return (g / (1.0 + jnp.exp(-g)) * u).astype(BF16)

    def sum_b(h, t):
        v = pb[h, x, t].astype(F32)
        for d in (1, 2, 3):
            v = v + rb[h, mod4(x - d), t].astype(F32)
        return v

    def second_b(h):
        for d in (1, 3, 2):
            arrived(rb.at[h, mod4(x - d)], h, "rsb", d)
        sbf[h] = sum_b(h, 1 - zl).astype(BF16)
        send(sbf.at[h], rb2.at[h], h, "rsb2", 0, partner)

    def hidden(h):
        arrived(rb2.at[h], h, "rsb2", 0)
        hb[h, zh, zl, :, WA:COLS] = swiglu(sum_b(h, zl) + rb2[h].astype(F32), WB)
        for d in (1, 3, 2):
            arrived(ra2.at[h, mod4(x - d)], h, "rsa2", d)
        va = pa[h, x, zl].astype(F32) + ra[h, x].astype(F32)
        for d in (1, 2, 3):
            va = va + ra2[h, mod4(x - d)].astype(F32)
        hb[h, zh, zl, :, 0:WA] = swiglu(va, WA)

    def gram(h, row, flipped, panel, total, w):
        def flip(i, _):
            lanes = pl.ds(pl.multiple_of(i * 2 * R, 2 * R), 2 * R)
            flipped[:, lanes] = jnp.transpose(row[h, i].reshape(2 * R, w))
            return 0

        lax.fori_loop(0, 4, flip, 0)

        def step(i, _):
            cc, n = i // (w // 256), lax.rem(i, w // 256)
            here = pl.ds(pl.multiple_of(n * 256, 256), 256)
            there = pl.ds(pl.multiple_of(i * 256, 256), 256)
            right = panel[h, cc, :, :, :, here].reshape(8 * R, 256)
            v = jnp.dot(flipped[...], right, preferred_element_type=F32) * (1.0 / TOTAL)
            if h:
                v = v + total[:, there]
            total[:, there] = v
            return 0

        lax.fori_loop(0, 2 * w // 256, step, 0)

    def store(src, dst):
        copy = pltpu.make_async_copy(src, dst, osem.at[len(outs)])
        copy.start()
        outs.append(copy)

    def step_zw(h):
        z_wait(h, "z", raw)
        if h + 2 < NH:
            z_send(h + 2, "z", raw)
        column_first(h, "X", raw, xc)
        squares(h)

    def step_sc(h):
        scales(h)
        normalize(h, raw.at[h, zh], nb.at[h], zh, y)
        row_first(h, "X", nb.at[h], xf)

    def step_p(h, d):
        if (h, d) == (0, 0):
            for copy in w_copies:
                copy.wait()
        products(h, d)

    def step_hid(h):
        hidden(h)
        z_send(h, "Hz", hb)
        row_first(h, "H", hb.at[h, zh], hf)

    def step_hz(h):
        z_wait(h, "Hz", hb)
        column_first(h, "H", hb, hc)

    def step_hl(h):
        for d in (0, 1, 3, 2):
            column_done(h, "H", hs, d)
        row_done(h, "H", hf)
        gram(h, hf, hft, hs, ghid, COLS)

    def step_gx(h):
        row_done(h, "X", xf)
        gram(h, xf, xft, xs, gin, FEAT)
        if h == NH - 1:
            store(gin, gin_out)

    named = {
        "ZW": step_zw,
        "SC": step_sc,
        "C2": lambda h: column_second(h, "X", xc, xs),
        "C3": lambda h, d: column_third(h, "X", xs, d),
        "P": step_p,
        "R2": lambda h: row_second(h, "X", nb.at[h], xf),
        "R3": lambda h: row_third(h, "X", xf),
        "S": second,
        "SB": second_b,
        "HID": step_hid,
        "HZ": step_hz,
        "HC2": lambda h: column_second(h, "H", hc, hs),
        "HR2": lambda h: row_second(h, "H", hb.at[h, zh], hf),
        "HR3": lambda h: row_third(h, "H", hf),
        "HC3": lambda h, d: column_third(h, "H", hs, d),
        "HL": step_hl,
        "GX": step_gx,
    }
    for h in range(min(2, NH)):
        z_send(h, "z", raw)
    for step in ORDER:
        name, *places = step.split(":")
        named[name](*[int(place) for place in places])
    store(ghid, ghid_out)
    for copy in pending:
        copy.wait_send()
    for copy in outs:
        copy.wait()


def grams(tokens, lang, gain, gate_weight, up_weight):
    def vm(*shape, dtype=BF16):
        return pltpu.VMEM(shape, dtype)

    any_spec = pl.BlockSpec(memory_space=pl.ANY)
    vmem_spec = pl.BlockSpec(memory_space=pltpu.VMEM)
    scratch = [
        vm(NH, 2, 2, R, FEAT), vm(NH, 2, R, FEAT), vm(NH, 8, 8, 2 * R, dtype=F32), vm(NH, 2 * R, 128, dtype=F32),
        vm(NH, 4, 2, R, FEAT), vm(NH, 4, 2, R, FEAT), vm(NH, 2, 4, 2, R, FEAT),
        vm(DEPTH, COLS), vm(DEPTH, COLS),
        vm(NH, 4, 2, R, 2 * WA), vm(NH, 4, 2, R, 2 * WB),
        vm(NH, 4, R, 2 * WA), vm(NH, 4, R, 2 * WA),
        vm(NH, 4, 2, R, 2 * WB), vm(NH, R, 2 * WB), vm(NH, R, 2 * WB),
        vm(NH, 2, 2, R, COLS), vm(NH, 4, 2, R, COLS), vm(NH, 4, 2, R, COLS), vm(NH, 2, 4, 2, R, COLS),
        vm(FEAT, 8 * R), vm(COLS, 8 * R),
        vm(FEAT, 2 * FEAT, dtype=F32), vm(COLS, 2 * COLS, dtype=F32),
        pltpu.SemaphoreType.DMA((NH * PER_PART,)), pltpu.SemaphoreType.DMA((NH * PER_PART,)),
        pltpu.SemaphoreType.DMA((2,)), pltpu.SemaphoreType.DMA((2,)),
    ]
    return pl.pallas_call(
        kernel,
        out_shape=[
            jax.ShapeDtypeStruct((FEAT, 2 * FEAT), F32),
            jax.ShapeDtypeStruct((COLS, 2 * COLS), F32),
        ],
        in_specs=[vmem_spec, vmem_spec, vmem_spec, any_spec, any_spec],
        out_specs=[any_spec] * 2,
        scratch_shapes=scratch,
        compiler_params=pltpu.CompilerParams(
            collective_id=0, has_side_effects=True, vmem_limit_bytes=60 * 2**20
        ),
        cost_estimate=pl.CostEstimate(flops=13 * 10**9, bytes_accessed=10 * 2**20, transcendentals=0),
    )(tokens, lang, gain, gate_weight, up_weight)


def per_device(tokens, lang_ids, norm_gain, gate_weight, up_weight):
    gain = norm_gain.reshape(16, 1, FEAT)
    return tuple(grams(tokens, lang_ids.reshape(TOK // 128, 128), gain, gate_weight, up_weight))


def solution(mesh):
    in_specs = (P("seq", "fsdp"), P("seq"), P(), P("seq", "fsdp"), P("seq", "fsdp"))
    out_specs = (P("fsdp", "seq"), P("fsdp", "seq"))
    return jax.shard_map(
        per_device, mesh=mesh, in_specs=in_specs, out_specs=out_specs, check_vma=False
    )
```

```python
import jax
import jax.numpy as jnp
from jax import lax
from jax.experimental import pallas as pl
from jax.experimental.pallas import tpu as pltpu
from jax.sharding import PartitionSpec as P

MESH = pl.DeviceIdType.MESH
F32 = jnp.float32
BF16 = jnp.bfloat16
TOK = 256
FEAT = 512
COLS = 768
WA, WB = 512, 256
DEPTH = 1024
TOTAL = 2048
D = 8192
NH = 4
R = TOK // NH
ORDER = (
    "ZN:0", "RX:3", "ZA:0", "Y:0", "ZN:1", "RX:0", "SC:0", "ZN:3", "RX:1", "R2:0", "ZN:2", "ZA:1", "Y:1", "RX:2",
    "R2:1", "C2:0", "ZA:3", "Y:3", "SC:1", "R2:3", "R3:0", "C2:1", "ZA:2", "C3:0:1", "C3:0:3", "P:0:0", "Y:2",
    "P:0:1", "C3:0:2", "SC:3", "P:0:3", "C2:3", "P:1:0", "C3:1:2", "C3:1:1", "P:1:1", "P:0:2", "P:3:0", "C3:1:3",
    "SC:2", "C2:2", "SB:0", "C3:3:1", "P:2:0", "S:1:0", "S:0:3", "S:0:2", "P:1:2", "S:0:1", "C3:2:1", "P:1:3",
    "S:0:0", "C3:2:2", "C3:3:2", "S:3:0", "P:2:1", "C3:2:3", "P:2:2", "S:1:3", "S:1:1", "S:1:2", "P:2:3",
    "HID:0", "P:3:2", "S:2:2", "S:2:3", "R2:2", "SB:1", "HR1:0", "S:2:0", "S:2:1", "S:3:2", "HZ:0", "P:3:1",
    "HID:1", "HR1:1", "GX:0", "R3:1", "C3:3:3", "P:3:3", "SB:2", "S:3:1", "HC2:0", "HR2:0", "HZ:1", "HID:2",
    "S:3:3", "GX:1", "HC2:1", "SB:3", "HR3:0", "HR1:2", "HID:3", "HC3:0:3", "R3:2", "HZ:2", "HC3:0:1", "HR1:3",
    "HC3:1:1", "HR2:1", "HZ:3", "HR2:2", "HC2:2", "R3:3", "HC3:0:2", "HR3:1", "GX:2", "HR2:3", "HL:0", "HC2:3",
    "HC3:1:3", "HR3:2", "HC3:2:1", "HC3:2:3", "HC3:1:2", "HC3:2:2", "GX:3", "HL:1", "HC3:3:3", "HC3:3:1",
    "HR3:3", "HC3:3:2", "HL:2", "HL:3",
)

_RANGES = {}
_next = 0
for _name, _count in (
    ("z", 3), ("ss", 8), ("sx", 4), ("rsa", 4), ("rsb", 4), ("rsa2", 4), ("rsb2", 1),
    ("Xcy", 4), ("Xrx", 4), ("Xax", 4), ("Xsib", 4), ("Xrz", 4),
    ("Hz", 3), ("Hcy", 4), ("Hrx", 4), ("Hax", 4), ("Hsib", 4), ("Hrz", 4),
):
    _RANGES[_name] = _next
    _next += _count
PER_PART = _next


def mod4(v):
    return lax.rem(v + 8, 4)


def kernel(
    tok_ref, lang_ref, gain_ref, wg_hbm, wu_hbm,
    gin_out, ghid_out, left_out, right_out,
    raw, ss, srow, xc, xf, xs, wg, wu, pa, pb, ra, ra2, rb, rb2, sbf,
    hb, hc, hf, hs, xft, hft, gin, ghid,
    ssem, rsem, wsem, osem,
):
    f = lax.axis_index("fsdp")
    s = lax.axis_index("seq")
    zh, y, c = f // 8, lax.rem(f // 2, 4), lax.rem(f, 2)
    zl, x = s // 4, lax.rem(s, 4)

    def dev(zh_, y_, c_, zl_, x_):
        return (zh_ * 8 + y_ * 2 + c_, zl_ * 4 + x_)

    z_src = [(zh, 1 - zl), (1 - zh, zl), (1 - zh, 1 - zl)]
    z_peers = [dev(a, y, c, b, x) for a, b in z_src]
    partner = z_peers[0]
    sib = dev(zh, y, 1 - c, zl, x)

    def x_peer(d):
        return dev(zh, y, c, zl, mod4(x + d))

    def y_peer(d, e=0):
        return dev(zh, mod4(y + d), c if e == 0 else 1 - c, zl, x)

    pending = []
    outs = []

    def remote(src, dst, h, name, i, device):
        at = h * PER_PART + _RANGES[name] + i
        return pltpu.make_async_remote_copy(
            src_ref=src, dst_ref=dst, send_sem=ssem.at[at], recv_sem=rsem.at[at],
            device_id=device, device_id_type=MESH,
        )

    def send(src, dst, h, name, i, device):
        copy = remote(src, dst, h, name, i, device)
        copy.start()
        pending.append((h, name, copy))

    def sent(h=None, name=None):
        for entry in list(pending):
            if name is None or entry[:2] == (h, name):
                entry[2].wait_send()
                pending.remove(entry)

    def arrived(dst, h, name, i):
        remote(dst, dst, h, name, i, sib).wait_recv()

    w_copies = [
        pltpu.make_async_copy(wg_hbm, wg, wsem.at[0]),
        pltpu.make_async_copy(wu_hbm, wu, wsem.at[1]),
    ]
    for copy in w_copies:
        copy.start()

    barrier = pltpu.get_barrier_semaphore()
    peers = list(z_peers) + [x_peer(d) for d in (1, 2, 3)]
    peers += [y_peer(d, e) for d in range(4) for e in range(2) if (d, e) != (0, 0)]
    for peer in peers:
        pl.semaphore_signal(barrier, inc=1, device_id=peer, device_id_type=MESH)
    keep = (lang_ref[...] == 0).astype(F32)
    for i in range(TOK // 128):
        col = jnp.transpose(jnp.broadcast_to(keep[i:i + 1], (128, 128)))
        for k in range(FEAT // 128):
            lanes = slice(k * 128, (k + 1) * 128)
            v = (tok_ref[i * 128:(i + 1) * 128, lanes].astype(F32) * col).astype(BF16)
            for j in range(128 // R):
                raw[i * (128 // R) + j, zh, zl, :, lanes] = v[j * R:(j + 1) * R]
    pl.semaphore_wait(barrier, len(peers))

    def z_send(h, name, own):
        for i, peer in enumerate(z_peers):
            send(own.at[h, zh, zl], own.at[h, zh, zl], h, name, i, peer)

    def z_wait(h, name, own):
        for i, (a, b) in enumerate(z_src):
            arrived(own.at[h, a, b], h, name, i)

    slot = y * 2 + c

    def squares(h):
        v0 = raw[h, 0].reshape(2 * R, FEAT).astype(F32)
        v1 = raw[h, 1].reshape(2 * R, FEAT).astype(F32)
        sq = v0 * v0 + v1 * v1
        sq = sq[:, 0:128] + sq[:, 128:256] + sq[:, 256:384] + sq[:, 384:512]
        row = jnp.sum(jnp.transpose(sq), axis=0, keepdims=True)
        ss[h, slot] = jnp.broadcast_to(row, (8, 2 * R))
        for d in range(4):
            for e in range(2):
                if (d, e) != (0, 0):
                    send(ss.at[h, slot], ss.at[h, slot], h, "ss", d * 2 + e, y_peer(d, e))

    def scales(h):
        for d in range(4):
            for e in range(2):
                if (d, e) != (0, 0):
                    at = mod4(y - d) * 2 + (c if e == 0 else 1 - c)
                    arrived(ss.at[h, at], h, "ss", d * 2 + e)
        total = ss[h, 0]
        for i in range(1, 8):
            total = total + ss[h, i]
        srow[h, x] = lax.rsqrt(total / float(D) + 1e-05)
        for d in (1, 3, 2):
            send(srow.at[h, x], srow.at[h, x], h, "sx", d, x_peer(d))

    def scale_columns(h, xx):
        return jnp.transpose(jnp.broadcast_to(srow[h, xx, 0:1], (128, 2 * R)))

    def normalize(part, col, b, yy):
        g = gain_ref[b * 8 + yy * 2 + c]
        for k in range(FEAT // 128):
            lanes = slice(k * 128, (k + 1) * 128)
            v = part[:, :, lanes].reshape(2 * R, 128).astype(F32)
            part[:, :, lanes] = (v * col * g[:, lanes]).astype(BF16).reshape(2, R, 128)

    def row_first(h, q, own, row):
        for d in (1, 3):
            send(own.at[h, zh, zl], row.at[h, x, zl], h, q + "rx", d, x_peer(d))

    def column_first(h, q, own, col):
        for d in (1, 3, 2):
            send(own.at[h, zl], col.at[h, y], h, q + "cy", d, y_peer(d))
        col[h, y] = own[h, zl]

    def column_wait(h, q, col, yy, scale):
        d = mod4(y - yy)

        @pl.when(d != 0)
        def _():
            arrived(col.at[h, yy], h, q + "cy", d)

        if q == "X":
            normalize(col.at[h, yy], scale, zl, yy)

    def column_second(h, q, col, panel):
        scale = scale_columns(h, x) if q == "X" else None
        for d in (1, 3, 2):
            to = mod4(x + d)
            column_wait(h, q, col, to, scale)
            send(col.at[h, to], panel.at[h, c, x], h, q + "ax", d, x_peer(d))
        column_wait(h, q, col, x, scale)
        send(col.at[h, x], panel.at[h, c, x], h, q + "sib", 0, sib)
        panel[h, c, x] = col[h, x]

    def column_third(h, q, panel, d):
        at = mod4(x - d)
        arrived(panel.at[h, c, at], h, q + "ax", d)
        send(panel.at[h, c, at], panel.at[h, c, at], h, q + "sib", d, sib)

    def column_done(h, q, panel, d):
        arrived(panel.at[h, 1 - c, mod4(x - d)], h, q + "sib", d)

    def row_second(h, q, own, row):
        row[h, x] = own[h, zh]
        for d, half in ((1, 0), (3, 1)):
            at = mod4(x - d)
            arrived(row.at[h, at, zl], h, q + "rx", d)
            rows = pl.ds(half * (R // 2), R // 2)
            send(row.at[h, at, zl, rows], row.at[h, at, zl, rows], h, q + "rx", 2 * half, x_peer(d))
            send(row.at[h, at, zl], row.at[h, at, zl], h, q + "rz", d, partner)

    def row_third(h, q, row):
        at = mod4(x - 2)
        for half in range(2):
            arrived(row.at[h, at, zl, pl.ds(half * (R // 2), R // 2)], h, q + "rx", 2 * half)
        send(row.at[h, at, zl], row.at[h, at, zl], h, q + "rz", 2, partner)

    def row_done(h, q, row):
        for d in (1, 3, 2):
            arrived(row.at[h, mod4(x - d), 1 - zl], h, q + "rz", d)

    def products(h, d):
        column_done(h, "X", xs, d)
        at = mod4(x - d)
        a0 = xs[h, 0, at].reshape(2 * R, FEAT)
        a1 = xs[h, 1, at].reshape(2 * R, FEAT)

        def product(w, lanes):
            v = jnp.dot(a0, w[0:FEAT, lanes], preferred_element_type=F32)
            v = v + jnp.dot(a1, w[FEAT:DEPTH, lanes], preferred_element_type=F32)
            return v.astype(BF16).reshape(2, R, 256)

        def step(n, _):
            here = pl.ds(pl.multiple_of(n * 256, 256), 256)
            there = pl.ds(pl.multiple_of(WA + n * 256, 256), 256)
            pa[h, at, :, :, here] = product(wg, here)
            pa[h, at, :, :, there] = product(wu, here)
            return 0

        lax.fori_loop(0, WA // 256, step, 0)
        send(pa.at[h, at, 1 - zl], ra.at[h, at], h, "rsa", d, partner)
        pb[h, at, :, :, 0:WB] = product(wg, slice(WA, COLS))
        pb[h, at, :, :, WB:2 * WB] = product(wu, slice(WA, COLS))
        if d:
            send(pb.at[h, at], rb.at[h, x], h, "rsb", 4 - d, dev(zh, y, c, zl, at))

    def second(h, d):
        at = mod4(x - d)
        arrived(ra.at[h, at], h, "rsa", d)
        if d:
            pa[h, at, zl] = (pa[h, at, zl].astype(F32) + ra[h, at].astype(F32)).astype(BF16)
            send(pa.at[h, at, zl], ra2.at[h, x], h, "rsa2", 4 - d, dev(zh, y, c, zl, at))

    def swiglu(v, w):
        g, u = v[:, 0:w], v[:, w:2 * w]
        return (g / (1.0 + jnp.exp(-g)) * u).astype(BF16)

    def sum_b(h, t):
        v = pb[h, x, t].astype(F32)
        for d in (1, 2, 3):
            v = v + rb[h, mod4(x - d), t].astype(F32)
        return v

    def second_b(h):
        for d in (1, 3, 2):
            arrived(rb.at[h, mod4(x - d)], h, "rsb", d)
        sbf[h] = sum_b(h, 1 - zl).astype(BF16)
        send(sbf.at[h], rb2.at[h], h, "rsb2", 0, partner)

    def hidden(h):
        arrived(rb2.at[h], h, "rsb2", 0)
        hb[h, zh, zl, :, WA:COLS] = swiglu(sum_b(h, zl) + rb2[h].astype(F32), WB)
        for d in (1, 3, 2):
            arrived(ra2.at[h, mod4(x - d)], h, "rsa2", d)
        va = pa[h, x, zl].astype(F32) + ra[h, x].astype(F32)
        for d in (1, 2, 3):
            va = va + ra2[h, mod4(x - d)].astype(F32)
        hb[h, zh, zl, :, 0:WA] = swiglu(va, WA)

    def gram(h, row, flipped, panel, total, w):
        def flip(i, _):
            lanes = pl.ds(pl.multiple_of(i * 2 * R, 2 * R), 2 * R)
            flipped[:, lanes] = jnp.transpose(row[h, i].reshape(2 * R, w))
            return 0

        lax.fori_loop(0, 4, flip, 0)
        if total is ghid and h == NH - 1:
            store(flipped, left_out)
            for cc in range(2):
                store(panel.at[h, cc], right_out.at[:, :, :, pl.ds(cc * w, w)])
            return

        def step(i, _):
            cc, n = i // (w // 256), lax.rem(i, w // 256)
            here = pl.ds(pl.multiple_of(n * 256, 256), 256)
            there = pl.ds(pl.multiple_of(i * 256, 256), 256)
            right = panel[h, cc, :, :, :, here].reshape(8 * R, 256)
            v = jnp.dot(flipped[...], right, preferred_element_type=F32) * (1.0 / TOTAL)
            if h:
                v = v + total[:, there]
            total[:, there] = v
            return 0

        lax.fori_loop(0, 2 * w // 256, step, 0)
        if total is ghid and h == NH - 2:
            store(ghid, ghid_out)

    def store(src, dst):
        copy = pltpu.make_async_copy(src, dst, osem.at[len(outs)])
        copy.start()
        outs.append(copy)

    def step_za(h):
        z_wait(h, "z", raw)
        squares(h)

    def step_p(h, d):
        if (h, d) == (0, 0):
            for copy in w_copies:
                copy.wait()
        products(h, d)

    def step_hid(h):
        hidden(h)
        z_send(h, "Hz", hb)

    def step_hz(h):
        z_wait(h, "Hz", hb)
        column_first(h, "H", hb, hc)

    def step_hl(h):
        for d in (0, 1, 3, 2):
            column_done(h, "H", hs, d)
        row_done(h, "H", hf)
        gram(h, hf, hft, hs, ghid, COLS)

    def step_gx(h):
        row_done(h, "X", xf)
        sent(h, "Xrx")
        sent(h, "Xrz")
        for d in (0, 1, 3, 2):
            at = mod4(x - d)
            if d:
                arrived(srow.at[h, at], h, "sx", d)
            normalize(xf.at[h, at], scale_columns(h, at), zh, y)
        gram(h, xf, xft, xs, gin, FEAT)
        if h == NH - 1:
            store(gin, gin_out)

    named = {
        "ZN": lambda h: z_send(h, "z", raw),
        "RX": lambda h: row_first(h, "X", raw, xf),
        "ZA": step_za,
        "Y": lambda h: column_first(h, "X", raw, xc),
        "SC": scales,
        "C2": lambda h: column_second(h, "X", xc, xs),
        "C3": lambda h, d: column_third(h, "X", xs, d),
        "P": step_p,
        "R2": lambda h: row_second(h, "X", raw, xf),
        "R3": lambda h: row_third(h, "X", xf),
        "S": second,
        "SB": second_b,
        "HID": step_hid,
        "HR1": lambda h: row_first(h, "H", hb, hf),
        "HZ": step_hz,
        "HC2": lambda h: column_second(h, "H", hc, hs),
        "HR2": lambda h: row_second(h, "H", hb, hf),
        "HR3": lambda h: row_third(h, "H", hf),
        "HC3": lambda h, d: column_third(h, "H", hs, d),
        "HL": step_hl,
        "GX": step_gx,
    }
    for step in ORDER:
        name, *places = step.split(":")
        named[name](*[int(place) for place in places])
    sent()
    for copy in outs:
        copy.wait()


def grams(tokens, lang, gain, gate_weight, up_weight):
    def vm(*shape, dtype=BF16):
        return pltpu.VMEM(shape, dtype)

    any_spec = pl.BlockSpec(memory_space=pl.ANY)
    vmem_spec = pl.BlockSpec(memory_space=pltpu.VMEM)
    scratch = [
        vm(NH, 2, 2, R, FEAT), vm(NH, 8, 8, 2 * R, dtype=F32), vm(NH, 4, 8, 2 * R, dtype=F32),
        vm(NH, 4, 2, R, FEAT), vm(NH, 4, 2, R, FEAT), vm(NH, 2, 4, 2, R, FEAT),
        vm(DEPTH, COLS), vm(DEPTH, COLS),
        vm(NH, 4, 2, R, 2 * WA), vm(NH, 4, 2, R, 2 * WB),
        vm(NH, 4, R, 2 * WA), vm(NH, 4, R, 2 * WA),
        vm(NH, 4, 2, R, 2 * WB), vm(NH, R, 2 * WB), vm(NH, R, 2 * WB),
        vm(NH, 2, 2, R, COLS), vm(NH, 4, 2, R, COLS), vm(NH, 4, 2, R, COLS), vm(NH, 2, 4, 2, R, COLS),
        vm(FEAT, 8 * R), vm(COLS, 8 * R),
        vm(FEAT, 2 * FEAT, dtype=F32), vm(COLS, 2 * COLS, dtype=F32),
        pltpu.SemaphoreType.DMA((NH * PER_PART,)), pltpu.SemaphoreType.DMA((NH * PER_PART,)),
        pltpu.SemaphoreType.DMA((2,)), pltpu.SemaphoreType.DMA((5,)),
    ]
    shapes = [
        ((FEAT, 2 * FEAT), F32), ((COLS, 2 * COLS), F32),
        ((COLS, 8 * R), BF16), ((4, 2, R, 2 * COLS), BF16),
    ]
    return pl.pallas_call(
        kernel,
        out_shape=[jax.ShapeDtypeStruct(shape, dtype) for shape, dtype in shapes],
        in_specs=[vmem_spec, vmem_spec, vmem_spec, any_spec, any_spec],
        out_specs=[any_spec] * 4,
        scratch_shapes=scratch,
        compiler_params=pltpu.CompilerParams(
            collective_id=0, has_side_effects=True, vmem_limit_bytes=60 * 2**20
        ),
        cost_estimate=pl.CostEstimate(flops=13 * 10**9, bytes_accessed=10 * 2**20, transcendentals=0),
    )(tokens, lang, gain, gate_weight, up_weight)


def last_kernel(gin, ghid, left, right, gin_out, ghid_out):
    v = jnp.dot(left[...], right[...], preferred_element_type=F32) * (1.0 / TOTAL)
    ghid_out[...] = ghid[...] + v
    gin_out[...] = gin[...]


def last_part(gin, ghid, left, right):
    n = 8

    def rows(a):
        return pl.BlockSpec((a.shape[0] // n, a.shape[1]), lambda i: (i, 0))

    return pl.pallas_call(
        last_kernel,
        grid=(n,),
        out_shape=[jax.ShapeDtypeStruct(a.shape, F32) for a in (gin, ghid)],
        in_specs=[rows(gin), rows(ghid), rows(left), pl.BlockSpec(right.shape, lambda i: (0, 0))],
        out_specs=[rows(gin), rows(ghid)],
        compiler_params=pltpu.CompilerParams(vmem_limit_bytes=60 * 2**20),
        cost_estimate=pl.CostEstimate(
            flops=2 * COLS * 2 * COLS * 8 * R, bytes_accessed=16 * 2**20, transcendentals=0
        ),
    )(gin, ghid, left, right)


def per_device(tokens, lang_ids, norm_gain, gate_weight, up_weight):
    gain = norm_gain.reshape(16, 1, FEAT)
    lang = lang_ids.reshape(TOK // 128, 128)
    gin, ghid, left, right = grams(tokens, lang, gain, gate_weight, up_weight)
    return tuple(last_part(gin, ghid, left, right.reshape(8 * R, 2 * COLS)))


def solution(mesh):
    in_specs = (P("seq", "fsdp"), P("seq"), P(), P("seq", "fsdp"), P("seq", "fsdp"))
    out_specs = (P("fsdp", "seq"), P("fsdp", "seq"))
    return jax.shard_map(
        per_device, mesh=mesh, in_specs=in_specs, out_specs=out_specs, check_vma=False
    )
```

```python
import jax
import jax.numpy as jnp
from jax import lax
from jax.experimental import pallas as pl
from jax.experimental.pallas import tpu as pltpu
from jax.sharding import PartitionSpec as P

MESH = pl.DeviceIdType.MESH
F32 = jnp.float32
BF16 = jnp.bfloat16
TOK = 256
FEAT = 512
COLS = 768
WA, WB = 512, 256
DEPTH = 1024
TOTAL = 2048
D = 8192
NH = 4
R = TOK // NH
ORDER = (
    "ZN:0", "ZA:0", "ZN:2", "Y:0", "RX:2", "RX:1", "RX:3", "SC:0", "ZN:3", "ZA:2", "Y:2", "ZN:1", "RX:0", "R2:2",
    "C2:0", "ZA:3", "R3:2", "Y:3", "R2:0", "SC:2", "ZA:1", "R2:1", "C2:2", "Y:1", "SC:3", "R3:0", "C3:0:3",
    "C3:0:1", "P:0:0", "P:2:0", "C2:3", "P:0:3", "C3:0:2", "C3:2:1", "SC:1", "C2:1", "P:0:1", "C3:2:3", "C3:2:2",
    "P:0:2", "P:2:1", "P:2:2", "C3:3:3", "C3:3:2", "P:2:3", "S:2:0", "PB:0", "C3:3:1", "C3:1:3", "S:0:1",
    "P:1:0", "C3:1:2", "C3:1:1", "S:0:3", "S:0:2", "PB:2", "S:0:0", "P:1:3", "GX:0", "P:3:2", "SB:0", "P:1:1",
    "S:2:2", "P:1:2", "S:2:3", "SA:0", "HID:0", "PB:1", "S:3:2", "P:3:3", "SB:2", "S:1:3", "S:1:2", "HR1:0",
    "P:3:1", "S:1:1", "S:2:1", "SA:2", "PB:3", "HZ:0", "R3:1", "SA:1", "HID:2", "HR1:2", "S:1:0", "S:3:1",
    "S:3:3", "P:3:0", "GX:1", "SB:1", "SA:3", "HZ:2", "R2:3", "HC2:0", "SB:3", "HID:1", "GX:2", "S:3:0", "HR1:1",
    "HC2:2", "HID:3", "R3:3", "HZ:1", "HC3:0:2", "HR1:3", "HR2:2", "HR2:1", "HR2:0", "HZ:3", "GX:3", "HC2:1",
    "HC3:2:3", "HR3:2", "HR3:0", "HC3:2:1", "HC3:0:3", "HC2:3", "HR3:1", "HC3:0:1", "HC3:1:3", "HR2:3",
    "HC3:2:2", "HC3:1:1", "HC3:1:2", "HL:0", "HL:1", "HR3:3", "HC3:3:1", "HC3:3:3", "HC3:3:2", "HL:2", "HL:3",
)

_RANGES = {}
_next = 0
for _name, _count in (
    ("z", 3), ("ss", 8), ("sx", 4), ("rsa", 4), ("rsb", 4), ("rsa2", 4), ("rsb2", 1),
    ("Xcy", 4), ("Xrx", 4), ("Xax", 4), ("Xsib", 4), ("Xrz", 4),
    ("Hz", 3), ("Hcy", 4), ("Hrx", 4), ("Hax", 4), ("Hsib", 4), ("Hrz", 4),
):
    _RANGES[_name] = _next
    _next += _count
PER_PART = _next


def mod4(v):
    return lax.rem(v + 8, 4)


def kernel(
    tok_ref, lang_ref, gain_ref, wg_hbm, wu_hbm,
    gin_out, ghid_out, left_out, right_out,
    raw, ss, srow, xc, xf, xs, wg, wu, pa, pf, pz, pb, ra, rah, ra2, rb, rbh, rb2, sbf,
    hb, hc, hf, hs, xft, hft, gin, ghid,
    ssem, rsem, wsem, osem,
):
    f = lax.axis_index("fsdp")
    s = lax.axis_index("seq")
    zh, y, c = f // 8, lax.rem(f // 2, 4), lax.rem(f, 2)
    zl, x = s // 4, lax.rem(s, 4)

    def dev(zh_, y_, c_, zl_, x_):
        return (zh_ * 8 + y_ * 2 + c_, zl_ * 4 + x_)

    z_src = [(zh, 1 - zl), (1 - zh, zl), (1 - zh, 1 - zl)]
    z_peers = [dev(a, y, c, b, x) for a, b in z_src]
    partner = z_peers[0]
    sib = dev(zh, y, 1 - c, zl, x)

    def x_peer(d):
        return dev(zh, y, c, zl, mod4(x + d))

    def y_peer(d, e=0):
        return dev(zh, mod4(y + d), c if e == 0 else 1 - c, zl, x)

    pending = []
    outs = []

    def remote(src, dst, h, name, i, device):
        at = h * PER_PART + _RANGES[name] + i
        return pltpu.make_async_remote_copy(
            src_ref=src, dst_ref=dst, send_sem=ssem.at[at], recv_sem=rsem.at[at],
            device_id=device, device_id_type=MESH,
        )

    def send(src, dst, h, name, i, device):
        copy = remote(src, dst, h, name, i, device)
        copy.start()
        pending.append((h, name, copy))

    def sent(h=None, name=None):
        for entry in list(pending):
            if name is None or entry[:2] == (h, name):
                entry[2].wait_send()
                pending.remove(entry)

    def arrived(dst, h, name, i):
        remote(dst, dst, h, name, i, sib).wait_recv()

    w_copies = [
        pltpu.make_async_copy(wg_hbm, wg, wsem.at[0]),
        pltpu.make_async_copy(wu_hbm, wu, wsem.at[1]),
    ]
    for copy in w_copies:
        copy.start()

    barrier = pltpu.get_barrier_semaphore()
    peers = list(z_peers) + [x_peer(d) for d in (1, 2, 3)]
    peers += [y_peer(d, e) for d in range(4) for e in range(2) if (d, e) != (0, 0)]
    for peer in peers:
        pl.semaphore_signal(barrier, inc=1, device_id=peer, device_id_type=MESH)
    keep = (lang_ref[...] == 0).astype(F32)
    for i in range(TOK // 128):
        col = jnp.transpose(jnp.broadcast_to(keep[i:i + 1], (128, 128)))
        for k in range(FEAT // 128):
            lanes = slice(k * 128, (k + 1) * 128)
            v = (tok_ref[i * 128:(i + 1) * 128, lanes].astype(F32) * col).astype(BF16)
            for j in range(128 // R):
                raw[i * (128 // R) + j, zh, zl, :, lanes] = v[j * R:(j + 1) * R]
    pl.semaphore_wait(barrier, len(peers))

    def z_send(h, name, own):
        for i, peer in enumerate(z_peers):
            send(own.at[h, zh, zl], own.at[h, zh, zl], h, name, i, peer)

    def z_wait(h, name, own):
        for i, (a, b) in enumerate(z_src):
            arrived(own.at[h, a, b], h, name, i)

    slot = y * 2 + c

    def squares(h):
        v0 = raw[h, 0].reshape(2 * R, FEAT).astype(F32)
        v1 = raw[h, 1].reshape(2 * R, FEAT).astype(F32)
        sq = v0 * v0 + v1 * v1
        sq = sq[:, 0:128] + sq[:, 128:256] + sq[:, 256:384] + sq[:, 384:512]
        row = jnp.sum(jnp.transpose(sq), axis=0, keepdims=True)
        ss[h, slot] = jnp.broadcast_to(row, (8, 2 * R))
        for d in range(4):
            for e in range(2):
                if (d, e) != (0, 0):
                    send(ss.at[h, slot], ss.at[h, slot], h, "ss", d * 2 + e, y_peer(d, e))

    def scales(h):
        for d in range(4):
            for e in range(2):
                if (d, e) != (0, 0):
                    at = mod4(y - d) * 2 + (c if e == 0 else 1 - c)
                    arrived(ss.at[h, at], h, "ss", d * 2 + e)
        total = ss[h, 0]
        for i in range(1, 8):
            total = total + ss[h, i]
        srow[h, x] = lax.rsqrt(total / float(D) + 1e-05)
        for d in (1, 3, 2):
            send(srow.at[h, x], srow.at[h, x], h, "sx", d, x_peer(d))

    def scale_columns(h, xx):
        return jnp.transpose(jnp.broadcast_to(srow[h, xx, 0:1], (128, 2 * R)))

    def normalize(part, col, b, yy):
        g = gain_ref[b * 8 + yy * 2 + c]
        for k in range(FEAT // 128):
            lanes = slice(k * 128, (k + 1) * 128)
            v = part[:, :, lanes].reshape(2 * R, 128).astype(F32)
            part[:, :, lanes] = (v * col * g[:, lanes]).astype(BF16).reshape(2, R, 128)

    def row_first(h, q, own, row):
        for d in (1, 3):
            send(own.at[h, zh, zl], row.at[h, x, zl], h, q + "rx", d, x_peer(d))

    def column_first(h, q, own, col):
        for d in (1, 3, 2):
            send(own.at[h, zl], col.at[h, y], h, q + "cy", d, y_peer(d))
        col[h, y] = own[h, zl]

    def column_wait(h, q, col, yy, scale):
        d = mod4(y - yy)

        @pl.when(d != 0)
        def _():
            arrived(col.at[h, yy], h, q + "cy", d)

        if q == "X":
            normalize(col.at[h, yy], scale, zl, yy)

    def column_second(h, q, col, panel):
        scale = scale_columns(h, x) if q == "X" else None
        for d in (1, 3, 2):
            to = mod4(x + d)
            column_wait(h, q, col, to, scale)
            send(col.at[h, to], panel.at[h, c, x], h, q + "ax", d, x_peer(d))
        column_wait(h, q, col, x, scale)
        send(col.at[h, x], panel.at[h, c, x], h, q + "sib", 0, sib)
        panel[h, c, x] = col[h, x]

    def column_third(h, q, panel, d):
        at = mod4(x - d)
        arrived(panel.at[h, c, at], h, q + "ax", d)
        send(panel.at[h, c, at], panel.at[h, c, at], h, q + "sib", d, sib)

    def column_done(h, q, panel, d):
        arrived(panel.at[h, 1 - c, mod4(x - d)], h, q + "sib", d)

    def row_second(h, q, own, row):
        row[h, x] = own[h, zh]
        for d, half in ((1, 0), (3, 1)):
            at = mod4(x - d)
            arrived(row.at[h, at, zl], h, q + "rx", d)
            rows = pl.ds(half * (R // 2), R // 2)
            send(row.at[h, at, zl, rows], row.at[h, at, zl, rows], h, q + "rx", 2 * half, x_peer(d))
            send(row.at[h, at, zl], row.at[h, at, zl], h, q + "rz", d, partner)

    def row_third(h, q, row):
        at = mod4(x - 2)
        for half in range(2):
            arrived(row.at[h, at, zl, pl.ds(half * (R // 2), R // 2)], h, q + "rx", 2 * half)
        send(row.at[h, at, zl], row.at[h, at, zl], h, q + "rz", 2, partner)

    def row_done(h, q, row):
        for d in (1, 3, 2):
            arrived(row.at[h, mod4(x - d), 1 - zl], h, q + "rz", d)

    def products(h, d):
        column_done(h, "X", xs, d)
        at = mod4(x - d)
        a0 = xs[h, 0, at].reshape(2 * R, FEAT)
        a1 = xs[h, 1, at].reshape(2 * R, FEAT)

        def product(w, lanes):
            v = jnp.dot(a0, w[0:FEAT, lanes], preferred_element_type=F32)
            v = v + jnp.dot(a1, w[FEAT:DEPTH, lanes], preferred_element_type=F32)
            return v.reshape(2, R, 256)

        def keep_a(v, lanes):
            pf[h, at, :, lanes] = jnp.where(zl == 0, v[0], v[1])
            pa[h, at, :, lanes] = jnp.where(zl == 0, v[1], v[0]).astype(BF16)

        def step(n, _):
            here = pl.ds(pl.multiple_of(n * 256, 256), 256)
            there = pl.ds(pl.multiple_of(WA + n * 256, 256), 256)
            keep_a(product(wg, here), here)
            keep_a(product(wu, here), there)
            return 0

        lax.fori_loop(0, WA // 256, step, 0)
        send(pa.at[h, at], ra.at[h, at], h, "rsa", d, partner)
        pb[h, at, :, :, 0:WB] = product(wg, slice(WA, COLS)).astype(BF16)
        pb[h, at, :, :, WB:2 * WB] = product(wu, slice(WA, COLS)).astype(BF16)
        if d == 2:
            send(pb.at[h, at, 0], rbh.at[h, 0], h, "rsb", 2, x_peer(1))
            send(pb.at[h, at, 1], rbh.at[h, 1], h, "rsb", 0, x_peer(3))

    def pass_b(h):
        for half, d in ((0, 1), (1, 3)):
            at = mod4(x + d)
            arrived(rbh.at[h, half], h, "rsb", 2 - 2 * half)
            pb[h, at, half] = (pb[h, at, half].astype(F32) + rbh[h, half].astype(F32)).astype(BF16)
            send(pb.at[h, at], rb.at[h, half], h, "rsb", d, x_peer(d))

    def second(h, d):
        at = mod4(x - d)
        arrived(ra.at[h, at], h, "rsa", d)
        if d == 2:
            pz[h, 2] = (pf[h, at] + ra[h, at].astype(F32)).astype(BF16)
            for half, e in ((0, 1), (1, 3)):
                rows = pl.ds(half * (R // 2), R // 2)
                send(pz.at[h, 2, rows], rah.at[h, half], h, "rsa2", 2 - 2 * half, x_peer(e))

    def pass_a(h):
        for half, d in ((0, 1), (1, 3)):
            at = mod4(x + d)
            arrived(rah.at[h, half], h, "rsa2", 2 - 2 * half)
            for part in range(2):
                rows = slice(part * (R // 2), (part + 1) * (R // 2))
                v = pf[h, at, rows] + ra[h, at, rows].astype(F32)
                if part == half:
                    v = v + rah[h, half].astype(F32)
                pz[h, half, rows] = v.astype(BF16)
            send(pz.at[h, half], ra2.at[h, half], h, "rsa2", d, x_peer(d))

    def swiglu(v, w):
        g, u = v[:, 0:w], v[:, w:2 * w]
        return (g / (1.0 + jnp.exp(-g)) * u).astype(BF16)

    def sum_b(h, t):
        v = pb[h, x, t].astype(F32)
        return v + rb[h, 0, t].astype(F32) + rb[h, 1, t].astype(F32)

    def second_b(h):
        for half, d in ((0, 1), (1, 3)):
            arrived(rb.at[h, half], h, "rsb", d)
        sbf[h] = sum_b(h, 1 - zl).astype(BF16)
        send(sbf.at[h], rb2.at[h], h, "rsb2", 0, partner)

    def hidden(h):
        arrived(rb2.at[h], h, "rsb2", 0)
        hb[h, zh, zl, :, WA:COLS] = swiglu(sum_b(h, zl) + rb2[h].astype(F32), WB)
        for half, d in ((0, 1), (1, 3)):
            arrived(ra2.at[h, half], h, "rsa2", d)
        va = pf[h, x] + ra[h, x].astype(F32)
        va = va + ra2[h, 0].astype(F32) + ra2[h, 1].astype(F32)
        hb[h, zh, zl, :, 0:WA] = swiglu(va, WA)

    def gram(h, row, flipped, panel, total, w):
        def flip(i, _):
            lanes = pl.ds(pl.multiple_of(i * 2 * R, 2 * R), 2 * R)
            flipped[:, lanes] = jnp.transpose(row[h, i].reshape(2 * R, w))
            return 0

        lax.fori_loop(0, 4, flip, 0)
        if total is ghid and h == NH - 1:
            store(flipped, left_out)
            for cc in range(2):
                store(panel.at[h, cc], right_out.at[:, :, :, pl.ds(cc * w, w)])
            return

        def step(i, _):
            cc, n = i // (w // 256), lax.rem(i, w // 256)
            here = pl.ds(pl.multiple_of(n * 256, 256), 256)
            there = pl.ds(pl.multiple_of(i * 256, 256), 256)
            right = panel[h, cc, :, :, :, here].reshape(8 * R, 256)
            v = jnp.dot(flipped[...], right, preferred_element_type=F32) * (1.0 / TOTAL)
            if h:
                v = v + total[:, there]
            total[:, there] = v
            return 0

        lax.fori_loop(0, 2 * w // 256, step, 0)
        if total is ghid and h == NH - 2:
            store(ghid, ghid_out)

    def store(src, dst):
        copy = pltpu.make_async_copy(src, dst, osem.at[len(outs)])
        copy.start()
        outs.append(copy)

    def step_za(h):
        z_wait(h, "z", raw)
        squares(h)

    def step_p(h, d):
        if (h, d) == (0, 0):
            for copy in w_copies:
                copy.wait()
        products(h, d)

    def step_hid(h):
        hidden(h)
        z_send(h, "Hz", hb)

    def step_hz(h):
        z_wait(h, "Hz", hb)
        column_first(h, "H", hb, hc)

    def step_hl(h):
        for d in (0, 1, 3, 2):
            column_done(h, "H", hs, d)
        row_done(h, "H", hf)
        gram(h, hf, hft, hs, ghid, COLS)

    def step_gx(h):
        row_done(h, "X", xf)
        sent(h, "Xrx")
        sent(h, "Xrz")
        for d in (0, 1, 3, 2):
            at = mod4(x - d)
            if d:
                arrived(srow.at[h, at], h, "sx", d)
            normalize(xf.at[h, at], scale_columns(h, at), zh, y)
        gram(h, xf, xft, xs, gin, FEAT)
        if h == NH - 1:
            store(gin, gin_out)

    named = {
        "ZN": lambda h: z_send(h, "z", raw),
        "RX": lambda h: row_first(h, "X", raw, xf),
        "ZA": step_za,
        "Y": lambda h: column_first(h, "X", raw, xc),
        "SC": scales,
        "C2": lambda h: column_second(h, "X", xc, xs),
        "C3": lambda h, d: column_third(h, "X", xs, d),
        "P": step_p,
        "R2": lambda h: row_second(h, "X", raw, xf),
        "R3": lambda h: row_third(h, "X", xf),
        "S": second,
        "PB": pass_b,
        "SA": pass_a,
        "SB": second_b,
        "HID": step_hid,
        "HR1": lambda h: row_first(h, "H", hb, hf),
        "HZ": step_hz,
        "HC2": lambda h: column_second(h, "H", hc, hs),
        "HR2": lambda h: row_second(h, "H", hb, hf),
        "HR3": lambda h: row_third(h, "H", hf),
        "HC3": lambda h, d: column_third(h, "H", hs, d),
        "HL": step_hl,
        "GX": step_gx,
    }
    for step in ORDER:
        name, *places = step.split(":")
        named[name](*[int(place) for place in places])
    sent()
    for copy in outs:
        copy.wait()


def grams(tokens, lang, gain, gate_weight, up_weight):
    def vm(*shape, dtype=BF16):
        return pltpu.VMEM(shape, dtype)

    any_spec = pl.BlockSpec(memory_space=pl.ANY)
    vmem_spec = pl.BlockSpec(memory_space=pltpu.VMEM)
    scratch = [
        vm(NH, 2, 2, R, FEAT), vm(NH, 8, 8, 2 * R, dtype=F32), vm(NH, 4, 8, 2 * R, dtype=F32),
        vm(NH, 4, 2, R, FEAT), vm(NH, 4, 2, R, FEAT), vm(NH, 2, 4, 2, R, FEAT),
        vm(DEPTH, COLS), vm(DEPTH, COLS),
        vm(NH, 4, R, 2 * WA), vm(NH, 4, R, 2 * WA, dtype=F32), vm(NH, 3, R, 2 * WA), vm(NH, 4, 2, R, 2 * WB),
        vm(NH, 4, R, 2 * WA), vm(NH, 2, R // 2, 2 * WA), vm(NH, 2, R, 2 * WA),
        vm(NH, 2, 2, R, 2 * WB), vm(NH, 2, R, 2 * WB), vm(NH, R, 2 * WB), vm(NH, R, 2 * WB),
        vm(NH, 2, 2, R, COLS), vm(NH, 4, 2, R, COLS), vm(NH, 4, 2, R, COLS), vm(NH, 2, 4, 2, R, COLS),
        vm(FEAT, 8 * R), vm(COLS, 8 * R),
        vm(FEAT, 2 * FEAT, dtype=F32), vm(COLS, 2 * COLS, dtype=F32),
        pltpu.SemaphoreType.DMA((NH * PER_PART,)), pltpu.SemaphoreType.DMA((NH * PER_PART,)),
        pltpu.SemaphoreType.DMA((2,)), pltpu.SemaphoreType.DMA((5,)),
    ]
    shapes = [
        ((FEAT, 2 * FEAT), F32), ((COLS, 2 * COLS), F32),
        ((COLS, 8 * R), BF16), ((4, 2, R, 2 * COLS), BF16),
    ]
    return pl.pallas_call(
        kernel,
        out_shape=[jax.ShapeDtypeStruct(shape, dtype) for shape, dtype in shapes],
        in_specs=[vmem_spec, vmem_spec, vmem_spec, any_spec, any_spec],
        out_specs=[any_spec] * 4,
        scratch_shapes=scratch,
        compiler_params=pltpu.CompilerParams(
            collective_id=0, has_side_effects=True, vmem_limit_bytes=60 * 2**20
        ),
        cost_estimate=pl.CostEstimate(flops=13 * 10**9, bytes_accessed=10 * 2**20, transcendentals=0),
    )(tokens, lang, gain, gate_weight, up_weight)


def last_kernel(gin, ghid, left, right, gin_out, ghid_out):
    v = jnp.dot(left[...], right[...], preferred_element_type=F32) * (1.0 / TOTAL)
    ghid_out[...] = ghid[...] + v
    gin_out[...] = gin[...]


def last_part(gin, ghid, left, right):
    n = 2

    def rows(a):
        return pl.BlockSpec((a.shape[0] // n, a.shape[1]), lambda i: (i, 0))

    return pl.pallas_call(
        last_kernel,
        grid=(n,),
        out_shape=[jax.ShapeDtypeStruct(a.shape, F32) for a in (gin, ghid)],
        in_specs=[rows(gin), rows(ghid), rows(left), pl.BlockSpec(right.shape, lambda i: (0, 0))],
        out_specs=[rows(gin), rows(ghid)],
        compiler_params=pltpu.CompilerParams(vmem_limit_bytes=60 * 2**20),
        cost_estimate=pl.CostEstimate(
            flops=2 * COLS * 2 * COLS * 8 * R, bytes_accessed=16 * 2**20, transcendentals=0
        ),
    )(gin, ghid, left, right)


def per_device(tokens, lang_ids, norm_gain, gate_weight, up_weight):
    gain = norm_gain.reshape(16, 1, FEAT)
    lang = lang_ids.reshape(TOK // 128, 128)
    gin, ghid, left, right = grams(tokens, lang, gain, gate_weight, up_weight)
    return tuple(last_part(gin, ghid, left, right.reshape(8 * R, 2 * COLS)))


def solution(mesh):
    in_specs = (P("seq", "fsdp"), P("seq"), P(), P("seq", "fsdp"), P("seq", "fsdp"))
    out_specs = (P("fsdp", "seq"), P("fsdp", "seq"))
    return jax.shard_map(
        per_device, mesh=mesh, in_specs=in_specs, out_specs=out_specs, check_vma=False
    )
```
